32 devices in a mesh: theta: 8 (over z, y), rad: 4 (over x, core).
Axes of the slice: x: 2, y: 2, z: 4, core: 2. Of those that a mesh axis runs over, the one named last changes fastest.
Arguments:
- flow_state: float32 [5, 7, 32, 32, 128], P(None, None, 'theta', 'rad'), may hold values from -6 to 16, as said below
- face_scale: float32 [32, 32, 128], P('theta', 'rad'), may hold values from 0.5 to 2
- volume: float32 [32, 32, 128], P('theta', 'rad'), may hold values from 0.5 to 2
- surface: float32 [9, 2048], P(None, ('theta', 'rad')), may hold values from -38 to 128, as said below
- centre_index: int32 [1024], P(('theta', 'rad')), may hold values from 0 to 2047, as said below
Outputs:
- residual: float32 [5, 7, 32, 32, 128], P(None, None, 'theta', 'rad')
The draws below stay inside these ranges and needn't reach their ends.
Inputs may be any that keep to these rules, and one draw needn't show every extreme that they name: `flow_state`: row 0 (density) and the pressure 0.4 (row 4 - |rows 1 to 3|^2 / (2 row 0)) are positive everywhere. `surface`: the positions lie on the 12 blades between hub and shroud radius and within the axial extent of the grid; the displacement coefficients are at most 2.5 in magnitude. `centre_index`: the 32 entries held by one device are distinct and name nodes of that device's own block of 64 columns of surface.
All inputs are finite; a program needn't handle non-finite values.
Results may differ from the reference program's by a relative error of at most 0.0003.
Values sent between devices are 32-bit elements; how exact they have to be, the bound alone decides.
A program may use at most 64 MiB of HBM per device.

```python
import math
import jax
import jax.numpy as jnp
import numpy as np
from jax import lax

NA = 128
TI = 7
NCEN = 1024
NSURF = 2048
BLADES = 12
NT = 32
NR = 32
NODE_DEV = 64
CEN_DEV = 32


def draw_flow_state(key, part):
    key = jax.random.fold_in(key, 11)
    keys = jax.random.split(key, 3)
    shape = (TI, NT, NR, NA)
    density = jnp.exp(jax.random.uniform(keys[0], shape, jnp.float32, -0.7, 0.7))
    motion = jnp.clip(0.5 * jax.random.normal(keys[1], (3,) + shape, jnp.float32), -1.5, 1.5)
    pressure = jnp.exp(jax.random.uniform(keys[2], shape, jnp.float32, -0.7, 0.7))
    momentum = density[None] * motion
    energy = pressure / 0.4 + 0.5 * density * jnp.sum(motion * motion, axis=0)
    return jnp.concatenate([density[None], momentum, energy[None]], axis=0)


def draw_surface(key, part):
    key = jax.random.fold_in(key, 23)
    keys = jax.random.split(key, 5)
    hub_radius = NT / (2.0 * math.pi)
    blade = jax.random.randint(keys[0], (NSURF,), 0, BLADES)
    span = jax.random.uniform(keys[1], (NSURF,), jnp.float32, 0.0, 1.0)
    height = jax.random.uniform(keys[2], (NSURF,), jnp.float32, 0.0, 1.0) * NA
    lean = jax.random.uniform(keys[3], (NSURF,), jnp.float32, -0.08, 0.08)
    angle = 2.0 * math.pi / BLADES * blade.astype(jnp.float32) + lean + 0.3 * height / NA
    radius = hub_radius + NR * span
    amplitude = 0.4
    weights = jnp.clip(amplitude * jax.random.normal(keys[4], (6, NSURF), jnp.float32), -5.0 * amplitude, 5.0 * amplitude)
    position = jnp.stack([radius * jnp.cos(angle), radius * jnp.sin(angle), height], axis=0)
    return jnp.concatenate([position, weights], axis=0)


def draw_centre_index(key, part):
    key = jax.random.fold_in(key, 37)
    blocks = NCEN // CEN_DEV
    keys = jax.random.split(key, blocks)
    picks = jax.vmap(lambda single: jax.random.permutation(single, NODE_DEV)[:CEN_DEV])(keys)
    return (picks + NODE_DEV * jnp.arange(blocks)[:, None]).reshape(NCEN).astype(jnp.int32)


def block_levels(key, extent, pieces, smallest, top_value):
    loudness = 1.0
    for axis_at, blocks in pieces:
        heights = jax.random.uniform(jax.random.fold_in(jax.random.fold_in(key, 6), axis_at), (blocks,), jnp.float32, smallest / len(pieces), top_value / len(pieces))
        loudness = loudness * jnp.repeat(jnp.exp(heights), extent[axis_at] // blocks).reshape((-1,) + (1,) * (len(extent) - 1 - axis_at))
    return loudness


def setup_inputs(seed: int = 0) -> dict:
    arg_keys = jax.random.split(jax.random.key(seed), 6)
    flow_state = draw_flow_state(jax.random.fold_in(arg_keys[5], 71), 0)
    face_scale = jnp.clip(jnp.exp(math.log(2.0) - 1.3862944 * jax.random.uniform(arg_keys[1], (NT, NR, NA), jnp.float32) ** block_levels(arg_keys[1], (NT, NR, NA), ((0, 8), (1, 4)), -0.2, 0.2)), 0.5, 2.0)
    volume = jnp.clip(jnp.exp(math.log(2.0) - 1.3862944 * jax.random.uniform(arg_keys[2], (NT, NR, NA), jnp.float32) ** block_levels(arg_keys[2], (NT, NR, NA), ((0, 8), (1, 4)), -0.2, 0.2)), 0.5, 2.0)
    surface = draw_surface(jax.random.fold_in(arg_keys[5], 71), 0)
    centre_index = draw_centre_index(jax.random.fold_in(arg_keys[5], 71), 0)
    return {"flow_state": flow_state, "face_scale": face_scale, "volume": volume, "surface": surface, "centre_index": centre_index}


heat_ratio = 1.4
frequency = 0.8
damping = 0.0625
support_radius = 4.0

def derivative_table(instances):
    values = np.zeros((instances, instances))
    for row_index in range(instances):
        for col_index in range(instances):
            if row_index != col_index:
                steps_apart = row_index - col_index
                values[row_index, col_index] = 0.5 * frequency * (-1.0) ** steps_apart / math.sin(math.pi * steps_apart / instances)
    return values

def base_points(angular, radial, axial, theta_cells):
    hub_radius = theta_cells / (2.0 * math.pi)
    angle = 2.0 * math.pi / theta_cells * (angular.astype(jnp.float32) + 0.5)
    radius = hub_radius + radial.astype(jnp.float32) + 0.5
    height = axial.astype(jnp.float32) + 0.5
    return jnp.stack(jnp.broadcast_arrays(radius * jnp.cos(angle), radius * jnp.sin(angle), height), axis=0)

def rbf_harmonics(points, centres, scale):
    squared = jnp.zeros((centres.shape[1], points.shape[1]), jnp.float32)
    for component in range(3):
        squared = squared + (points[component][None, :] - centres[component][:, None]) ** 2
    kernel = 1.0 / jnp.sqrt(1.0 + squared / (scale * scale))
    return jnp.dot(centres[3:], kernel, precision=lax.Precision.HIGHEST, preferred_element_type=jnp.float32)

def deformation(harmonics, base, derivative):
    instances = derivative.shape[0]
    phases = 2.0 * math.pi * np.arange(instances) / instances
    extra = (1,) * (harmonics.ndim - 1)
    cosine = jnp.asarray(np.cos(phases), jnp.float32).reshape((1, instances) + extra)
    sine = jnp.asarray(np.sin(phases), jnp.float32).reshape((1, instances) + extra)
    shift = harmonics[:3, None] * cosine + harmonics[3:, None] * sine
    coords = base[:, None] + shift
    velocity = jnp.einsum('nm,cm...->cn...', derivative, shift, precision=lax.Precision.HIGHEST)
    return (coords, velocity)

def extend_wrap(values, dim_index, layers):
    length = values.shape[dim_index]
    return jnp.concatenate([lax.slice_in_dim(values, length - layers, length, axis=dim_index), values, lax.slice_in_dim(values, 0, layers, axis=dim_index)], axis=dim_index)

def extend_edge(values, dim_index, layers):
    length = values.shape[dim_index]
    first_layer = lax.slice_in_dim(values, 0, 1, axis=dim_index)
    last_layer = lax.slice_in_dim(values, length - 1, length, axis=dim_index)
    return jnp.concatenate([first_layer] * layers + [values] + [last_layer] * layers, axis=dim_index)

def extend_line(values, dim_index):
    length = values.shape[dim_index]
    first_layer = lax.slice_in_dim(values, 0, 1, axis=dim_index)
    second_layer = lax.slice_in_dim(values, 1, 2, axis=dim_index)
    last_layer = lax.slice_in_dim(values, length - 1, length, axis=dim_index)
    before_last = lax.slice_in_dim(values, length - 2, length - 1, axis=dim_index)
    return jnp.concatenate([2.0 * first_layer - second_layer, values, 2.0 * last_layer - before_last], axis=dim_index)

def physical_flux(states, normal, grid_speed):
    density = states[0]
    momentum = states[1:4]
    speed = momentum / density
    pressure = (heat_ratio - 1.0) * (states[4] - 0.5 * lax.optimization_barrier(jnp.sum(momentum * speed, axis=0)))
    relative = lax.optimization_barrier(jnp.sum((speed - grid_speed) * normal, axis=0))
    return jnp.stack([density * relative, momentum[0] * relative + pressure * normal[0], momentum[1] * relative + pressure * normal[1], momentum[2] * relative + pressure * normal[2], states[4] * relative + pressure * lax.optimization_barrier(jnp.sum(speed * normal, axis=0))], axis=0)

def face_fluxes(states, coords, velocity, scales, dim_index):
    faces = coords.shape[dim_index] - 1

    def face_slice(values, offset, where_dim):
        return lax.slice_in_dim(values, offset, offset + faces, axis=where_dim)
    spacing = face_slice(coords, 1, dim_index) - face_slice(coords, 0, dim_index)
    length = jnp.sqrt(lax.optimization_barrier(jnp.sum(spacing * spacing, axis=0)))
    face_area = 0.5 * (face_slice(scales, 0, dim_index - 1) + face_slice(scales, 1, dim_index - 1))
    normal = spacing * (face_area / length)
    grid_speed = 0.5 * (face_slice(velocity, 0, dim_index) + face_slice(velocity, 1, dim_index))
    far_left = face_slice(states, 0, dim_index)
    left_state = face_slice(states, 1, dim_index)
    right_state = face_slice(states, 2, dim_index)
    far_right = face_slice(states, 3, dim_index)
    central = 0.5 * (physical_flux(left_state, normal, grid_speed) + physical_flux(right_state, normal, grid_speed))
    average = 0.5 * (left_state + right_state)
    mean_speed = average[1:4] / average[0]
    mean_pressure = (heat_ratio - 1.0) * (average[4] - 0.5 * lax.optimization_barrier(jnp.sum(average[1:4] * mean_speed, axis=0)))
    sound_speed = jnp.sqrt(heat_ratio * mean_pressure / average[0])
    spectral = jnp.abs(lax.optimization_barrier(jnp.sum((mean_speed - grid_speed) * normal, axis=0))) + sound_speed * face_area
    return central + damping * spectral * (far_right - 3.0 * right_state + 3.0 * left_state - far_left)

def reference(flow_state, face_scale, volume, surface, centre_index):
    variables, instances, theta_cells, radial_cells, axial_cells = flow_state.shape
    derivative = jnp.asarray(derivative_table(instances), jnp.float32)
    scale = support_radius
    centres = jnp.take(surface, centre_index, axis=1)
    base = base_points(jnp.arange(theta_cells).reshape(-1, 1, 1), jnp.arange(radial_cells).reshape(1, -1, 1), jnp.arange(axial_cells).reshape(1, 1, -1), theta_cells)
    rows = jnp.moveaxis(base.reshape(3, theta_cells, radial_cells * axial_cells), 1, 0)
    harmonics = lax.map(lambda points: rbf_harmonics(points, centres, scale), rows)
    harmonics = jnp.moveaxis(harmonics, 0, 1).reshape(6, theta_cells, radial_cells, axial_cells)
    coords, velocity = deformation(harmonics, base, derivative)

    def instance_residual(operands):
        states, positions, speeds = operands
        running = jnp.zeros_like(states)
        for dim_index in (1, 2, 3):
            if dim_index == 1:
                ext_states = extend_wrap(states, 1, 2)
                ext_positions = extend_wrap(positions, 1, 1)
                ext_speeds = extend_wrap(speeds, 1, 1)
                ext_scales = extend_wrap(face_scale, 0, 1)
            else:
                ext_states = extend_edge(states, dim_index, 2)
                ext_positions = extend_line(positions, dim_index)
                ext_speeds = extend_edge(speeds, dim_index, 1)
                ext_scales = extend_edge(face_scale, dim_index - 1, 1)
            fluxes = face_fluxes(ext_states, ext_positions, ext_speeds, ext_scales, dim_index)
            faces = fluxes.shape[dim_index]
            running = running + lax.slice_in_dim(fluxes, 1, faces, axis=dim_index) - lax.slice_in_dim(fluxes, 0, faces - 1, axis=dim_index)
        return running
    spatial = lax.map(instance_residual, (jnp.moveaxis(flow_state, 1, 0), jnp.moveaxis(coords, 1, 0), jnp.moveaxis(velocity, 1, 0)))
    temporal = jnp.einsum('nm,vm...->vn...', derivative, volume[None, None] * flow_state, precision=lax.Precision.HIGHEST)
    return temporal + jnp.moveaxis(spatial, 0, 1)
```

```python
import functools
import math

import jax
import jax.numpy as jnp
import numpy as np
from jax import lax
from jax.experimental import pallas as pl
from jax.experimental.pallas import tpu as pltpu
from jax.sharding import PartitionSpec as P

heat_ratio = 1.4
frequency = 0.8
damping = 0.0625
support_radius = 4.0
LANES = 128
MESH = pl.DeviceIdType.MESH


def derivative_table(instances):
    values = np.zeros((instances, instances))
    for row in range(instances):
        for col in range(instances):
            if row != col:
                steps = row - col
                values[row, col] = (
                    0.5 * frequency * (-1.0) ** steps / math.sin(math.pi * steps / instances)
                )
    return values


def constant_rows(instances, theta_total):
    phases = 2.0 * math.pi * np.arange(instances) / instances
    derivative = derivative_table(instances)
    rows = []
    for values in (np.cos(phases), np.sin(phases)):
        rows.append(np.resize(values, 8))
    for values in (np.cos(phases), np.sin(phases)):
        rows.append(np.resize(derivative @ values, 8))
    angle = 2.0 * math.pi / theta_total * (np.arange(theta_total) + 0.5)
    rows.append(np.cos(angle))
    rows.append(np.sin(angle))
    column = np.concatenate(rows).astype(np.float32)
    return np.ascontiguousarray(np.broadcast_to(column[:, None], (column.size, LANES)))


def dot3(a, b):
    return a[0] * b[0] + a[1] * b[1] + a[2] * b[2]


def face_flux(left, right, prim_l, prim_r, third, spacing, speed_sum, scale_sum):
    area = 0.5 * scale_sum
    factor = (0.5 * area) * lax.rsqrt(dot3(spacing, spacing))
    half = [s * factor for s in spacing]
    grid = 0.5 * dot3(speed_sum, half)
    un_l = dot3(prim_l, half)
    un_r = dot3(prim_r, half)
    q_l, q_r = un_l - grid, un_r - grid
    pressure = prim_l[3] + prim_r[3]
    flux = [left[v] * q_l + right[v] * q_r for v in range(5)]
    for c in range(3):
        flux[1 + c] = flux[1 + c] + pressure * half[c]
    flux[4] = flux[4] + prim_l[3] * un_l + prim_r[3] * un_r
    total = [left[v] + right[v] for v in range(5)]
    inverse = 1.0 / total[0]
    mean = [total[1 + c] * inverse for c in range(3)]
    sound2 = (heat_ratio * (heat_ratio - 1.0)) * (
        (total[4] - 0.5 * dot3(total[1:4], mean)) * inverse
    )
    spectral = 2.0 * jnp.abs(dot3(mean, half) - grid) + jnp.sqrt(sound2) * area
    weight = damping * spectral
    return [flux[v] + weight * third[v] for v in range(5)]


def end_flux(state, prim, third, spacing, speed, area):
    factor = area * lax.rsqrt(dot3(spacing, spacing))
    normal = [s * factor for s in spacing]
    un = dot3(prim, normal)
    q = un - dot3(speed, normal)
    flux = [state[v] * q for v in range(5)]
    for c in range(3):
        flux[1 + c] = flux[1 + c] + prim[3] * normal[c]
    flux[4] = flux[4] + prim[3] * un
    sound = jnp.sqrt(heat_ratio * prim[3] / state[0])
    weight = damping * (jnp.abs(q) + sound * area)
    return [flux[v] + weight * third[v] for v in range(5)]


def kernel(
    sizes,
    flow_ref,
    scale_ref,
    volume_ref,
    surface_ref,
    index_ref,
    table_ref,
    out_ref,
    own_pay,
    cent,
    weights,
    amat,
    bmat,
    hm,
    st,
    pr,
    xs,
    vs,
    sc,
    res,
    halo,
    gr_send,
    gr_recv,
    gt_send,
    gt_recv,
    st_send,
    st_recv,
    sr_send,
    sr_recv,
    ht_send,
    ht_recv,
    hr_send,
    hr_recv,
):
    nt, nr, variables, instances, tc, rc, cen = sizes
    th = lax.axis_index("theta")
    rd = lax.axis_index("rad")
    up, down = lax.rem(th + 1, nt), lax.rem(th + nt - 1, nt)
    lines = tc * rc
    plane = instances * lines
    flow_rows = flow_ref.reshape(variables * plane, LANES)
    halo_rows = halo.reshape(2 * variables * instances * 2 * rc, LANES)
    hub = nt * tc / (2.0 * math.pi)

    barrier = pltpu.get_barrier_semaphore()
    for d in range(1, nr):
        pl.semaphore_signal(
            barrier, inc=1, device_id={"rad": lax.rem(rd + d, nr)}, device_id_type=MESH
        )
    for d in range(1, nt):
        pl.semaphore_signal(
            barrier, inc=1, device_id={"theta": lax.rem(th + d, nt)}, device_id_type=MESH
        )

    per = LANES // (cen * nr)
    offset = (lax.rem(th, per) * nr + rd) * cen
    nodes = surface_ref.shape[1]
    ids = index_ref[...] - (th * nr + rd) * nodes
    chosen = (lax.broadcasted_iota(jnp.int32, (nodes, cen), 0) == ids).astype(jnp.float32)
    placed = (
        lax.broadcasted_iota(jnp.int32, (cen, LANES), 1)
        == lax.broadcasted_iota(jnp.int32, (cen, LANES), 0) + offset
    ).astype(jnp.float32)
    pay = jnp.dot(
        surface_ref[...], chosen, precision=lax.Precision.HIGHEST, preferred_element_type=jnp.float32
    )
    pay = jnp.dot(
        pay, placed, precision=lax.Precision.HIGHEST, preferred_element_type=jnp.float32
    )
    own_pay[rd] = jnp.zeros((16, LANES), jnp.float32)
    own_pay[rd, 0:6] = pay[3:9]
    own_pay[rd, 8:11] = pay[0:3]

    pl.semaphore_wait(barrier, nr - 1 + nt - 1)

    def rad_gather(d):
        peer = lax.rem(rd + d, nr)
        return pltpu.make_async_remote_copy(
            src_ref=own_pay.at[rd],
            dst_ref=own_pay.at[rd],
            send_sem=gr_send.at[d],
            recv_sem=gr_recv.at[d],
            device_id={"rad": peer},
            device_id_type=MESH,
        )

    rad_copies = [rad_gather(d) for d in range(1, nr)]
    for copy in rad_copies:
        copy.start()

    def state_theta(side):
        src = flow_ref.at[:, pl.ds((tc - 2) * rc if side == 0 else 0, 2 * rc), :]
        return pltpu.make_async_remote_copy(
            src_ref=src,
            dst_ref=halo.at[side],
            send_sem=st_send.at[side],
            recv_sem=st_recv.at[side],
            device_id={"theta": up if side == 0 else down},
            device_id_type=MESH,
        )

    theta_copies = [state_theta(0), state_theta(1)]

    def spread(source, base, v, i, j, stride):
        st[v, i, j, 0:instances] = source[pl.ds(base, instances, stride=stride), :]
        st[v, i, j, instances : instances + 1] = source[pl.ds(base, 1), :]

    def own_rows(step, carry):
        v, i = step // tc, step % tc
        for j in range(rc):
            spread(flow_rows, v * plane + i * rc + j, v, i + 2, j + 2, lines)
        return carry

    for copy in rad_copies:
        copy.wait_recv()
    block = own_pay[0]
    for r in range(1, nr):
        block = block + own_pay[r]
    cent[th] = block

    def theta_gather(d):
        peer = lax.rem(th + d, nt)
        return pltpu.make_async_remote_copy(
            src_ref=cent.at[th],
            dst_ref=cent.at[th],
            send_sem=gt_send.at[d],
            recv_sem=gt_recv.at[d],
            device_id={"theta": peer},
            device_id_type=MESH,
        )

    gather_copies = [theta_gather(d) for d in range(1, nt)]
    for copy in gather_copies:
        copy.start()
    for copy in theta_copies:
        copy.start()

    lax.fori_loop(0, variables * tc, own_rows, 0)

    def state_rad(side):
        src = pl.ds(rc, 2) if side == 0 else pl.ds(2, 2)
        dst = pl.ds(0, 2) if side == 0 else pl.ds(rc + 2, 2)
        return pltpu.make_async_remote_copy(
            src_ref=st.at[:, pl.ds(2, tc), src],
            dst_ref=st.at[:, pl.ds(2, tc), dst],
            send_sem=sr_send.at[side],
            recv_sem=sr_recv.at[side],
            device_id={"rad": lax.rem(rd + 1, nr) if side == 0 else lax.rem(rd + nr - 1, nr)},
            device_id_type=MESH,
        )

    rad_states = [state_rad(0), state_rad(1)]

    @pl.when(rd < nr - 1)
    def _():
        rad_states[0].start()

    @pl.when(rd > 0)
    def _():
        rad_states[1].start()

    def primitives(i, j):
        u = [st[v, i, j] for v in range(5)]
        inverse = 1.0 / u[0]
        speed = [u[1 + c] * inverse for c in range(3)]
        for c in range(3):
            pr[c, i, j] = speed[c]
        pr[3, i, j] = (heat_ratio - 1.0) * (u[4] - 0.5 * dot3(u[1:4], speed))

    inner = pl.ds(2, tc)

    def own_prims(j, carry):
        primitives(inner, j + 2)
        for v in range(5):
            res[v, pl.ds(1, tc + 2), j + 2] = jnp.zeros((tc + 2, 8, LANES), jnp.float32)
        return carry

    lax.fori_loop(0, rc, own_prims, 0)
    for j in (1, rc + 2):
        for v in range(5):
            res[v, inner, j] = jnp.zeros((tc, 8, LANES), jnp.float32)

    derivative = derivative_table(instances)

    def temporal(step, carry):
        v, i = step // tc, step % tc
        vol = volume_ref[pl.ds(pl.multiple_of(i * rc, rc), rc), :]
        first = v * plane + i * rc
        parts = [
            vol * flow_rows[pl.ds(pl.multiple_of(first + n * lines, 8), rc), :]
            for n in range(instances)
        ]
        for n in range(instances):
            value = 0.0
            for s in range(1, (instances + 1) // 2):
                value = value + float(derivative[s, 0]) * (
                    parts[(n - s) % instances] - parts[(n + s) % instances]
                )
            out_ref[pl.ds(pl.multiple_of(first + n * lines, 8), rc), :] = value
        return carry

    lax.fori_loop(0, variables * tc, temporal, 0)

    for copy in gather_copies:
        copy.wait_recv()

    blocks = nt // per
    radius8 = (
        lax.broadcasted_iota(jnp.int32, (rc, LANES), 0) + rd * rc
    ).astype(jnp.float32) + (hub + 0.5)
    height = lax.broadcasted_iota(jnp.int32, (LANES, LANES), 0).astype(jnp.float32) + 0.5
    inv_h = 1.0 / support_radius
    for b in range(blocks):
        group = cent[b * per]
        for q in range(1, per):
            group = group + cent[b * per + q]
        cols = slice(b * LANES, (b + 1) * LANES)
        w = group[0:8]
        high = w.astype(jnp.bfloat16)
        low = (w - high.astype(jnp.float32)).astype(jnp.bfloat16)
        weights[:, cols] = jnp.concatenate([high, low], axis=0)
        cx, cy, cz = group[8:9], group[9:10], group[10:11]
        dz = (height - cz) * inv_h
        bmat[:, cols] = dz * dz
        for i in range(tc):
            row = 32 + th * tc + i
            cosine = table_ref[pl.ds(row, 1), :]
            sine = table_ref[pl.ds(row + nt * tc, 1), :]
            dx = (radius8 * cosine - cx) * inv_h
            dy = (radius8 * sine - cy) * inv_h
            amat[i * rc : (i + 1) * rc, cols] = 1.0 + (dx * dx + dy * dy)

    row8 = lax.broadcasted_iota(jnp.int32, (8, LANES), 0)
    width = 2 * LANES
    total = blocks * LANES

    def line_sum(i, j):
        line = i * rc + j
        acc = jnp.zeros((16, LANES), jnp.float32)
        for m in range(0, total, width):
            cols = slice(m, m + width)
            rbf = lax.rsqrt(amat[pl.ds(line, 1), cols] + bmat[:, cols])
            high = rbf.astype(jnp.bfloat16)
            low = (rbf - high.astype(jnp.float32)).astype(jnp.bfloat16)
            for part in (high, low):
                acc = acc + lax.dot_general(
                    weights[:, cols], part, (((1,), (1,)), ((), ())),
                    preferred_element_type=jnp.float32,
                )
        values = acc[0:8] + acc[8:16]
        hm[i + 2, j + 2] = jnp.where(row8 == 6, scale_ref[pl.ds(line, 1), :], values)

    def outer_lines(step, carry):
        line_sum((step // rc) * (tc - 1), step % rc)
        return carry

    lax.fori_loop(0, 2 * rc, outer_lines, 0)

    def geometry_theta(side):
        src = tc + 1 if side == 0 else 2
        dst = 1 if side == 0 else tc + 2
        return pltpu.make_async_remote_copy(
            src_ref=hm.at[src, pl.ds(2, rc)],
            dst_ref=hm.at[dst, pl.ds(2, rc)],
            send_sem=ht_send.at[side],
            recv_sem=ht_recv.at[side],
            device_id={"theta": up if side == 0 else down},
            device_id_type=MESH,
        )

    theta_geometry = [geometry_theta(0), geometry_theta(1)]
    for copy in theta_geometry:
        copy.start()

    def side_lines(step, carry):
        line_sum(1 + step // 2, (step % 2) * (rc - 1))
        return carry

    lax.fori_loop(0, 2 * (tc - 2), side_lines, 0)

    def geometry_rad(side):
        src = rc + 1 if side == 0 else 2
        dst = 1 if side == 0 else rc + 2
        return pltpu.make_async_remote_copy(
            src_ref=hm.at[pl.ds(2, tc), src],
            dst_ref=hm.at[pl.ds(2, tc), dst],
            send_sem=hr_send.at[side],
            recv_sem=hr_recv.at[side],
            device_id={"rad": lax.rem(rd + 1, nr) if side == 0 else lax.rem(rd + nr - 1, nr)},
            device_id_type=MESH,
        )

    rad_geometry = [geometry_rad(0), geometry_rad(1)]

    @pl.when(rd < nr - 1)
    def _():
        rad_geometry[0].start()

    @pl.when(rd > 0)
    def _():
        rad_geometry[1].start()

    def middle_lines(step, carry):
        line_sum(1 + step // (rc - 2), 1 + step % (rc - 2))
        return carry

    lax.fori_loop(0, (tc - 2) * (rc - 2), middle_lines, 0)

    axial = lax.broadcasted_iota(jnp.int32, (8, LANES), 1).astype(jnp.float32) + 0.5

    def geometry(i, j):
        wave = hm[i, j]
        rows = [jnp.broadcast_to(wave[c : c + 1], (8, LANES)) for c in range(7)]
        cell = lax.rem(th * tc + i - 2 + nt * tc, nt * tc)
        radius = (rd * rc + j - 2).astype(jnp.float32) + (hub + 0.5)
        base = (
            radius * table_ref[pl.ds(32 + cell, 1), :],
            radius * table_ref[pl.ds(32 + nt * tc + cell, 1), :],
            axial,
        )
        for c in range(3):
            xs[c, i, j] = base[c] + (rows[c] * table_ref[0:8] + rows[3 + c] * table_ref[8:16])
            vs[c, i, j] = rows[c] * table_ref[16:24] + rows[3 + c] * table_ref[24:32]
        sc[i, j] = rows[6]

    def own_geometry(j, carry):
        for i in range(tc):
            geometry(i + 2, j + 2)
        return carry

    lax.fori_loop(0, rc, own_geometry, 0)

    first = lax.broadcasted_iota(jnp.int32, (tc, 8, LANES), 2) == 0
    last = lax.broadcasted_iota(jnp.int32, (tc, 8, LANES), 2) == LANES - 1

    def before(x):
        return pltpu.roll(x, 1, axis=2)

    def after(x):
        return pltpu.roll(x, LANES - 1, axis=2)

    def axial_faces(step, carry):
        j = step + 2
        right = [st[v, inner, j] for v in range(5)]
        left = [jnp.where(first, x, before(x)) for x in right]
        change = [r - l for r, l in zip(right, left)]
        third = [after(d) - 2.0 * d + jnp.where(first, 0.0, before(d)) for d in change]
        prim_r = [pr[c, inner, j] for c in range(4)]
        prim_l = [jnp.where(first, x, before(x)) for x in prim_r]
        spacing = []
        for c in range(3):
            x = xs[c, inner, j]
            s = x - before(x)
            spacing.append(jnp.where(first, after(s), s))
        speed = [vs[c, inner, j] for c in range(3)]
        speed_sum = [x + jnp.where(first, x, before(x)) for x in speed]
        area = sc[inner, j]
        area_sum = area + jnp.where(first, area, before(area))
        lower = face_flux(left, right, prim_l, prim_r, third, spacing, speed_sum, area_sum)
        end = end_flux(right, prim_r, change, spacing, speed, area)
        for v in range(5):
            res[v, inner, j] += jnp.where(last, end[v], after(lower[v])) - lower[v]
        return carry

    lax.fori_loop(0, rc, axial_faces, 0)

    def faces(cells):
        ll, l, r, rr = cells
        left = [st[(v, *l)] for v in range(5)]
        right = [st[(v, *r)] for v in range(5)]
        third = [
            (st[(v, *rr)] - st[(v, *ll)]) - 3.0 * (right[v] - left[v]) for v in range(5)
        ]
        flux = face_flux(
            left,
            right,
            [pr[(c, *l)] for c in range(4)],
            [pr[(c, *r)] for c in range(4)],
            third,
            [xs[(c, *r)] - xs[(c, *l)] for c in range(3)],
            [vs[(c, *r)] + vs[(c, *l)] for c in range(3)],
            sc[l] + sc[r],
        )
        for v in range(5):
            res[(v, *l)] += flux[v]
            res[(v, *r)] -= flux[v]

    half = rc // 2

    def theta_face(f, part):
        j = pl.ds(2 + part * half, half)
        faces([(f + k, j) for k in range(4)])

    def rad_face(f):
        faces([(inner, f + k) for k in range(4)])

    def theta_inner(step, carry):
        theta_face(2 + step // 2, step % 2)
        return carry

    def rad_inner(step, carry):
        rad_face(2 + step)
        return carry

    lax.fori_loop(0, 2 * (tc - 3), theta_inner, 0)
    lax.fori_loop(0, rc - 3, rad_inner, 0)

    for side in range(2):
        near, far, ghost = (2, 3, 1) if side == 0 else (rc + 1, rc, rc + 2)
        ghost2 = 0 if side == 0 else rc + 3
        at_end = (rd == 0) if side == 0 else (rd == nr - 1)

        @pl.when(at_end)
        def _():
            for v in range(5):
                value = st[v, inner, near]
                st[v, inner, ghost] = value
                st[v, inner, ghost2] = value
            for c in range(3):
                xs[c, inner, ghost] = 2.0 * xs[c, inner, near] - xs[c, inner, far]
                vs[c, inner, ghost] = vs[c, inner, near]
            sc[inner, ghost] = sc[inner, near]

        @pl.when(jnp.logical_not(at_end))
        def _():
            rad_states[side].wait_recv()
            rad_geometry[side].wait_recv()
            for i in range(tc):
                geometry(i + 2, ghost)

        primitives(inner, ghost)

    def rad_outer(step, carry):
        rad_face(step + (rc - 3) * (step // 2))
        return carry

    lax.fori_loop(0, 4, rad_outer, 0)

    for side in range(2):
        theta_geometry[side].wait_recv()
        theta_copies[side].wait_recv()

    def ghost_cells(step, carry):
        side, j = step // rc, step % rc
        for v in range(variables):
            for layer in range(2):
                start = ((side * variables + v) * instances * 2 + layer) * rc + j
                spread(halo_rows, start, v, side * (tc + 2) + layer, j + 2, 2 * rc)
        ghost = 1 + side * (tc + 1)
        geometry(ghost, j + 2)
        primitives(ghost, j + 2)
        return carry

    lax.fori_loop(0, 2 * rc, ghost_cells, 0)

    def theta_outer(step, carry):
        f = step // 2
        theta_face(f + (tc - 3) * (f // 2), step % 2)
        return carry

    lax.fori_loop(0, 8, theta_outer, 0)

    def finish(step, carry):
        v, i = step // tc, step % tc
        for j in range(rc):
            rows = pl.ds(v * plane + i * rc + j, instances, stride=lines)
            out_ref[rows, :] = out_ref[rows, :] + res[v, i + 2, j + 2, 0:instances]
        return carry

    lax.fori_loop(0, variables * tc, finish, 0)

    for copy in rad_copies + gather_copies + theta_copies + theta_geometry:
        copy.wait_send()

    @pl.when(rd < nr - 1)
    def _():
        rad_states[0].wait_send()
        rad_geometry[0].wait_send()

    @pl.when(rd > 0)
    def _():
        rad_states[1].wait_send()
        rad_geometry[1].wait_send()


def on_device(nt, nr, flow_state, face_scale, volume, surface, centre_index):
    variables, instances, tc, rc, na = flow_state.shape
    cen = centre_index.shape[0]
    sizes = (nt, nr, variables, instances, tc, rc, cen)
    table = jnp.asarray(constant_rows(instances, nt * tc))
    total = cen * nt * nr
    vmem = pl.BlockSpec(memory_space=pltpu.VMEM)
    f32 = jnp.float32
    cells = (tc + 4, rc + 4, 8, LANES)
    out = pl.pallas_call(
        functools.partial(kernel, sizes),
        out_shape=jax.ShapeDtypeStruct((variables * instances * tc * rc, na), f32),
        in_specs=[vmem] * 6,
        out_specs=vmem,
        scratch_shapes=[
            pltpu.VMEM((nr, 16, LANES), f32),
            pltpu.VMEM((nt, 16, LANES), f32),
            pltpu.VMEM((16, total), jnp.bfloat16),
            pltpu.VMEM((tc * rc, total), f32),
            pltpu.VMEM((LANES, total), f32),
            pltpu.VMEM(cells, f32),
            pltpu.VMEM((5,) + cells, f32),
            pltpu.VMEM((4,) + cells, f32),
            pltpu.VMEM((3,) + cells, f32),
            pltpu.VMEM((3,) + cells, f32),
            pltpu.VMEM(cells, f32),
            pltpu.VMEM((5,) + cells, f32),
            pltpu.VMEM((2, variables * instances, 2 * rc, LANES), f32),
            pltpu.SemaphoreType.DMA((nr,)),
            pltpu.SemaphoreType.DMA((nr,)),
            pltpu.SemaphoreType.DMA((nt,)),
            pltpu.SemaphoreType.DMA((nt,)),
        ]
        + [pltpu.SemaphoreType.DMA((2,))] * 8,
        compiler_params=pltpu.CompilerParams(
            collective_id=0, has_side_effects=True, vmem_limit_bytes=40 * 1024 * 1024
        ),
    )(
        flow_state.reshape(variables * instances, tc * rc, na),
        face_scale.reshape(tc * rc, na),
        volume.reshape(tc * rc, na),
        surface,
        centre_index.reshape(1, cen),
        table,
    )
    return out.reshape(flow_state.shape)


def solution(mesh):
    return jax.shard_map(
        functools.partial(on_device, mesh.shape["theta"], mesh.shape["rad"]),
        mesh=mesh,
        in_specs=(
            P(None, None, "theta", "rad", None),
            P("theta", "rad", None),
            P("theta", "rad", None),
            P(None, ("theta", "rad")),
            P(("theta", "rad")),
        ),
        out_specs=P(None, None, "theta", "rad", None),
        check_vma=False,
    )
```

```python
import functools
import math

import jax
import jax.numpy as jnp
import numpy as np
from jax import lax
from jax.experimental import pallas as pl
from jax.experimental.pallas import tpu as pltpu
from jax.sharding import PartitionSpec as P

heat_ratio = 1.4
frequency = 0.8
damping = 0.0625
support_radius = 4.0
LANES = 128
MESH = pl.DeviceIdType.MESH


def derivative_table(instances):
    values = np.zeros((instances, instances))
    for row in range(instances):
        for col in range(instances):
            if row != col:
                steps = row - col
                values[row, col] = (
                    0.5 * frequency * (-1.0) ** steps / math.sin(math.pi * steps / instances)
                )
    return values


def constant_rows(instances, theta_total):
    phases = 2.0 * math.pi * np.arange(instances) / instances
    derivative = derivative_table(instances)
    rows = []
    for values in (np.cos(phases), np.sin(phases)):
        rows.append(np.resize(values, 8))
    for values in (np.cos(phases), np.sin(phases)):
        rows.append(np.resize(derivative @ values, 8))
    angle = 2.0 * math.pi / theta_total * (np.arange(theta_total) + 0.5)
    rows.append(np.cos(angle))
    rows.append(np.sin(angle))
    column = np.concatenate(rows).astype(np.float32)
    return np.ascontiguousarray(np.broadcast_to(column[:, None], (column.size, LANES)))


def dot3(a, b):
    return a[0] * b[0] + a[1] * b[1] + a[2] * b[2]


def face_flux(left, right, prim_l, prim_r, third, spacing, speed_sum, scale_sum):
    area = 0.5 * scale_sum
    factor = (0.5 * area) * lax.rsqrt(dot3(spacing, spacing))
    half = [s * factor for s in spacing]
    grid = 0.5 * dot3(speed_sum, half)
    un_l = dot3(prim_l, half)
    un_r = dot3(prim_r, half)
    q_l, q_r = un_l - grid, un_r - grid
    pressure = prim_l[3] + prim_r[3]
    flux = [left[v] * q_l + right[v] * q_r for v in range(5)]
    for c in range(3):
        flux[1 + c] = flux[1 + c] + pressure * half[c]
    flux[4] = flux[4] + prim_l[3] * un_l + prim_r[3] * un_r
    total = [left[v] + right[v] for v in range(5)]
    inverse = 1.0 / total[0]
    mean = [total[1 + c] * inverse for c in range(3)]
    sound2 = (heat_ratio * (heat_ratio - 1.0)) * (
        (total[4] - 0.5 * dot3(total[1:4], mean)) * inverse
    )
    spectral = 2.0 * jnp.abs(dot3(mean, half) - grid) + jnp.sqrt(sound2) * area
    weight = damping * spectral
    return [flux[v] + weight * third[v] for v in range(5)]


def end_flux(state, prim, third, spacing, speed, area):
    factor = area * lax.rsqrt(dot3(spacing, spacing))
    normal = [s * factor for s in spacing]
    un = dot3(prim, normal)
    q = un - dot3(speed, normal)
    flux = [state[v] * q for v in range(5)]
    for c in range(3):
        flux[1 + c] = flux[1 + c] + prim[3] * normal[c]
    flux[4] = flux[4] + prim[3] * un
    sound = jnp.sqrt(heat_ratio * prim[3] / state[0])
    weight = damping * (jnp.abs(q) + sound * area)
    return [flux[v] + weight * third[v] for v in range(5)]


def kernel(
    sizes,
    flow_in,
    scale_in,
    volume_in,
    surface_in,
    index_in,
    table_in,
    out_ref,
    flow_ref,
    scale_ref,
    volume_ref,
    surface_ref,
    index_ref,
    table_ref,
    own_pay,
    cent,
    weights,
    amat,
    bmat,
    hm,
    st,
    pr,
    xs,
    vs,
    sc,
    res,
    halo,
    gr_send,
    gr_recv,
    gt_send,
    gt_recv,
    st_send,
    st_recv,
    sr_send,
    sr_recv,
    ht_send,
    ht_recv,
    hr_send,
    hr_recv,
    in_sem,
):
    nt, nr, variables, instances, tc, rc, cen = sizes
    th = lax.axis_index("theta")
    rd = lax.axis_index("rad")
    up, down = lax.rem(th + 1, nt), lax.rem(th + nt - 1, nt)
    lines = tc * rc
    plane = instances * lines
    flow_rows = flow_ref.reshape(variables * plane, LANES)
    halo_rows = halo.reshape(2 * variables * instances * 2 * rc, LANES)
    hub = nt * tc / (2.0 * math.pi)

    inputs = [
        pltpu.make_async_copy(src, dst, in_sem.at[k])
        for k, (src, dst) in enumerate(
            (
                (surface_in, surface_ref),
                (index_in, index_ref),
                (flow_in, flow_ref),
                (volume_in, volume_ref),
                (table_in, table_ref),
                (scale_in, scale_ref),
            )
        )
    ]
    for copy in inputs:
        copy.start()
    barrier = pltpu.get_barrier_semaphore()
    for d in range(1, nr):
        pl.semaphore_signal(
            barrier, inc=1, device_id={"rad": lax.rem(rd + d, nr)}, device_id_type=MESH
        )
    for d in range(1, nt):
        pl.semaphore_signal(
            barrier, inc=1, device_id={"theta": lax.rem(th + d, nt)}, device_id_type=MESH
        )

    for copy in inputs[:2]:
        copy.wait()

    per = LANES // (cen * nr)
    offset = (lax.rem(th, per) * nr + rd) * cen
    nodes = surface_ref.shape[1]
    ids = index_ref[...] - (th * nr + rd) * nodes
    chosen = (lax.broadcasted_iota(jnp.int32, (nodes, cen), 0) == ids).astype(jnp.float32)
    placed = (
        lax.broadcasted_iota(jnp.int32, (cen, LANES), 1)
        == lax.broadcasted_iota(jnp.int32, (cen, LANES), 0) + offset
    ).astype(jnp.float32)
    pay = jnp.dot(
        surface_ref[...], chosen, precision=lax.Precision.HIGHEST, preferred_element_type=jnp.float32
    )
    pay = jnp.dot(
        pay, placed, precision=lax.Precision.HIGHEST, preferred_element_type=jnp.float32
    )
    own_pay[rd] = jnp.zeros((16, LANES), jnp.float32)
    own_pay[rd, 0:6] = pay[3:9]
    own_pay[rd, 8:11] = pay[0:3]

    pl.semaphore_wait(barrier, nr - 1 + nt - 1)

    def rad_gather(d):
        peer = lax.rem(rd + d, nr)
        return pltpu.make_async_remote_copy(
            src_ref=own_pay.at[rd],
            dst_ref=own_pay.at[rd],
            send_sem=gr_send.at[d],
            recv_sem=gr_recv.at[d],
            device_id={"rad": peer},
            device_id_type=MESH,
        )

    rad_copies = [rad_gather(d) for d in range(1, nr)]
    for copy in rad_copies:
        copy.start()

    def state_theta(side):
        src = flow_ref.at[:, pl.ds((tc - 2) * rc if side == 0 else 0, 2 * rc), :]
        return pltpu.make_async_remote_copy(
            src_ref=src,
            dst_ref=halo.at[side],
            send_sem=st_send.at[side],
            recv_sem=st_recv.at[side],
            device_id={"theta": up if side == 0 else down},
            device_id_type=MESH,
        )

    theta_copies = [state_theta(0), state_theta(1)]

    def spread(source, base, v, i, j, stride):
        st[v, i, j, 0:instances] = source[pl.ds(base, instances, stride=stride), :]
        st[v, i, j, instances : instances + 1] = source[pl.ds(base, 1), :]

    def own_rows(step, carry):
        v, i = step // tc, step % tc
        for j in range(rc):
            spread(flow_rows, v * plane + i * rc + j, v, i + 2, j + 2, lines)
        return carry

    for copy in inputs[2:]:
        copy.wait()
    for copy in rad_copies:
        copy.wait_recv()
    block = own_pay[0]
    for r in range(1, nr):
        block = block + own_pay[r]
    cent[th] = block

    def theta_gather(d):
        peer = lax.rem(th + d, nt)
        return pltpu.make_async_remote_copy(
            src_ref=cent.at[th],
            dst_ref=cent.at[th],
            send_sem=gt_send.at[d],
            recv_sem=gt_recv.at[d],
            device_id={"theta": peer},
            device_id_type=MESH,
        )

    gather_copies = [theta_gather(d) for d in range(1, nt)]
    for copy in gather_copies:
        copy.start()
    for copy in theta_copies:
        copy.start()

    lax.fori_loop(0, variables * tc, own_rows, 0)

    def state_rad(side):
        src = pl.ds(rc, 2) if side == 0 else pl.ds(2, 2)
        dst = pl.ds(0, 2) if side == 0 else pl.ds(rc + 2, 2)
        return pltpu.make_async_remote_copy(
            src_ref=st.at[:, pl.ds(2, tc), src],
            dst_ref=st.at[:, pl.ds(2, tc), dst],
            send_sem=sr_send.at[side],
            recv_sem=sr_recv.at[side],
            device_id={"rad": lax.rem(rd + 1, nr) if side == 0 else lax.rem(rd + nr - 1, nr)},
            device_id_type=MESH,
        )

    rad_states = [state_rad(0), state_rad(1)]

    @pl.when(rd < nr - 1)
    def _():
        rad_states[0].start()

    @pl.when(rd > 0)
    def _():
        rad_states[1].start()

    def primitives(i, j):
        u = [st[v, i, j] for v in range(5)]
        inverse = 1.0 / u[0]
        speed = [u[1 + c] * inverse for c in range(3)]
        for c in range(3):
            pr[c, i, j] = speed[c]
        pr[3, i, j] = (heat_ratio - 1.0) * (u[4] - 0.5 * dot3(u[1:4], speed))

    inner = pl.ds(2, tc)

    def own_prims(j, carry):
        primitives(inner, j + 2)
        for v in range(5):
            res[v, pl.ds(1, tc + 2), j + 2] = jnp.zeros((tc + 2, 8, LANES), jnp.float32)
        return carry

    lax.fori_loop(0, rc, own_prims, 0)
    for j in (1, rc + 2):
        for v in range(5):
            res[v, inner, j] = jnp.zeros((tc, 8, LANES), jnp.float32)

    derivative = derivative_table(instances)

    def temporal(step, carry):
        v, i = step // tc, step % tc
        vol = volume_ref[pl.ds(pl.multiple_of(i * rc, rc), rc), :]
        first = v * plane + i * rc
        parts = [
            vol * flow_rows[pl.ds(pl.multiple_of(first + n * lines, 8), rc), :]
            for n in range(instances)
        ]
        for n in range(instances):
            value = 0.0
            for s in range(1, (instances + 1) // 2):
                value = value + float(derivative[s, 0]) * (
                    parts[(n - s) % instances] - parts[(n + s) % instances]
                )
            out_ref[pl.ds(pl.multiple_of(first + n * lines, 8), rc), :] = value
        return carry

    lax.fori_loop(0, variables * tc, temporal, 0)

    for copy in gather_copies:
        copy.wait_recv()

    blocks = nt // per
    radius8 = (
        lax.broadcasted_iota(jnp.int32, (rc, LANES), 0) + rd * rc
    ).astype(jnp.float32) + (hub + 0.5)
    height = lax.broadcasted_iota(jnp.int32, (LANES, LANES), 0).astype(jnp.float32) + 0.5
    inv_h = 1.0 / support_radius
    for b in range(blocks):
        group = cent[b * per]
        for q in range(1, per):
            group = group + cent[b * per + q]
        cols = slice(b * LANES, (b + 1) * LANES)
        w = group[0:8]
        high = w.astype(jnp.bfloat16)
        low = (w - high.astype(jnp.float32)).astype(jnp.bfloat16)
        weights[:, cols] = jnp.concatenate([high, low], axis=0)
        cx, cy, cz = group[8:9], group[9:10], group[10:11]
        dz = (height - cz) * inv_h
        bmat[:, cols] = dz * dz
        for i in range(tc):
            row = 32 + th * tc + i
            cosine = table_ref[pl.ds(row, 1), :]
            sine = table_ref[pl.ds(row + nt * tc, 1), :]
            dx = (radius8 * cosine - cx) * inv_h
            dy = (radius8 * sine - cy) * inv_h
            amat[i * rc : (i + 1) * rc, cols] = 1.0 + (dx * dx + dy * dy)

    row8 = lax.broadcasted_iota(jnp.int32, (8, LANES), 0)
    width = 2 * LANES
    total = blocks * LANES

    def line_sum(i, j):
        line = i * rc + j
        acc = jnp.zeros((16, LANES), jnp.float32)
        for m in range(0, total, width):
            cols = slice(m, m + width)
            rbf = lax.rsqrt(amat[pl.ds(line, 1), cols] + bmat[:, cols])
            high = rbf.astype(jnp.bfloat16)
            low = (rbf - high.astype(jnp.float32)).astype(jnp.bfloat16)
            for part in (high, low):
                acc = acc + lax.dot_general(
                    weights[:, cols], part, (((1,), (1,)), ((), ())),
                    preferred_element_type=jnp.float32,
                )
        values = acc[0:8] + acc[8:16]
        hm[i + 2, j + 2] = jnp.where(row8 == 6, scale_ref[pl.ds(line, 1), :], values)

    def outer_lines(step, carry):
        line_sum((step // rc) * (tc - 1), step % rc)
        return carry

    lax.fori_loop(0, 2 * rc, outer_lines, 0)

    def geometry_theta(side):
        src = tc + 1 if side == 0 else 2
        dst = 1 if side == 0 else tc + 2
        return pltpu.make_async_remote_copy(
            src_ref=hm.at[src, pl.ds(2, rc)],
            dst_ref=hm.at[dst, pl.ds(2, rc)],
            send_sem=ht_send.at[side],
            recv_sem=ht_recv.at[side],
            device_id={"theta": up if side == 0 else down},
            device_id_type=MESH,
        )

    theta_geometry = [geometry_theta(0), geometry_theta(1)]
    for copy in theta_geometry:
        copy.start()

    def side_lines(step, carry):
        line_sum(1 + step // 2, (step % 2) * (rc - 1))
        return carry

    lax.fori_loop(0, 2 * (tc - 2), side_lines, 0)

    def geometry_rad(side):
        src = rc + 1 if side == 0 else 2
        dst = 1 if side == 0 else rc + 2
        return pltpu.make_async_remote_copy(
            src_ref=hm.at[pl.ds(2, tc), src],
            dst_ref=hm.at[pl.ds(2, tc), dst],
            send_sem=hr_send.at[side],
            recv_sem=hr_recv.at[side],
            device_id={"rad": lax.rem(rd + 1, nr) if side == 0 else lax.rem(rd + nr - 1, nr)},
            device_id_type=MESH,
        )

    rad_geometry = [geometry_rad(0), geometry_rad(1)]

    @pl.when(rd < nr - 1)
    def _():
        rad_geometry[0].start()

    @pl.when(rd > 0)
    def _():
        rad_geometry[1].start()

    def middle_lines(step, carry):
        line_sum(1 + step // (rc - 2), 1 + step % (rc - 2))
        return carry

    lax.fori_loop(0, (tc - 2) * (rc - 2), middle_lines, 0)

    axial = lax.broadcasted_iota(jnp.int32, (8, LANES), 1).astype(jnp.float32) + 0.5

    def geometry(i, j):
        wave = hm[i, j]
        rows = [jnp.broadcast_to(wave[c : c + 1], (8, LANES)) for c in range(7)]
        cell = lax.rem(th * tc + i - 2 + nt * tc, nt * tc)
        radius = (rd * rc + j - 2).astype(jnp.float32) + (hub + 0.5)
        base = (
            radius * table_ref[pl.ds(32 + cell, 1), :],
            radius * table_ref[pl.ds(32 + nt * tc + cell, 1), :],
            axial,
        )
        for c in range(3):
            xs[c, i, j] = base[c] + (rows[c] * table_ref[0:8] + rows[3 + c] * table_ref[8:16])
            vs[c, i, j] = rows[c] * table_ref[16:24] + rows[3 + c] * table_ref[24:32]
        sc[i, j] = rows[6]

    def own_geometry(j, carry):
        for i in range(tc):
            geometry(i + 2, j + 2)
        return carry

    lax.fori_loop(0, rc, own_geometry, 0)

    first = lax.broadcasted_iota(jnp.int32, (tc, 8, LANES), 2) == 0
    last = lax.broadcasted_iota(jnp.int32, (tc, 8, LANES), 2) == LANES - 1

    def before(x):
        return pltpu.roll(x, 1, axis=2)

    def after(x):
        return pltpu.roll(x, LANES - 1, axis=2)

    def axial_faces(step, carry):
        j = step + 2
        right = [st[v, inner, j] for v in range(5)]
        left = [jnp.where(first, x, before(x)) for x in right]
        change = [r - l for r, l in zip(right, left)]
        third = [after(d) - 2.0 * d + jnp.where(first, 0.0, before(d)) for d in change]
        prim_r = [pr[c, inner, j] for c in range(4)]
        prim_l = [jnp.where(first, x, before(x)) for x in prim_r]
        spacing = []
        for c in range(3):
            x = xs[c, inner, j]
            s = x - before(x)
            spacing.append(jnp.where(first, after(s), s))
        speed = [vs[c, inner, j] for c in range(3)]
        speed_sum = [x + jnp.where(first, x, before(x)) for x in speed]
        area = sc[inner, j]
        area_sum = area + jnp.where(first, area, before(area))
        lower = face_flux(left, right, prim_l, prim_r, third, spacing, speed_sum, area_sum)
        end = end_flux(right, prim_r, change, spacing, speed, area)
        for v in range(5):
            res[v, inner, j] += jnp.where(last, end[v], after(lower[v])) - lower[v]
        return carry

    lax.fori_loop(0, rc, axial_faces, 0)

    def faces(cells):
        ll, l, r, rr = cells
        left = [st[(v, *l)] for v in range(5)]
        right = [st[(v, *r)] for v in range(5)]
        third = [
            (st[(v, *rr)] - st[(v, *ll)]) - 3.0 * (right[v] - left[v]) for v in range(5)
        ]
        flux = face_flux(
            left,
            right,
            [pr[(c, *l)] for c in range(4)],
            [pr[(c, *r)] for c in range(4)],
            third,
            [xs[(c, *r)] - xs[(c, *l)] for c in range(3)],
            [vs[(c, *r)] + vs[(c, *l)] for c in range(3)],
            sc[l] + sc[r],
        )
        for v in range(5):
            res[(v, *l)] += flux[v]
            res[(v, *r)] -= flux[v]

    half = rc // 2

    def theta_face(f, part):
        j = pl.ds(2 + part * half, half)
        faces([(f + k, j) for k in range(4)])

    def rad_face(f):
        faces([(inner, f + k) for k in range(4)])

    def theta_inner(step, carry):
        theta_face(2 + step // 2, step % 2)
        return carry

    def rad_inner(step, carry):
        rad_face(2 + step)
        return carry

    lax.fori_loop(0, 2 * (tc - 3), theta_inner, 0)
    lax.fori_loop(0, rc - 3, rad_inner, 0)

    for side in range(2):
        near, far, ghost = (2, 3, 1) if side == 0 else (rc + 1, rc, rc + 2)
        ghost2 = 0 if side == 0 else rc + 3
        at_end = (rd == 0) if side == 0 else (rd == nr - 1)

        @pl.when(at_end)
        def _():
            for v in range(5):
                value = st[v, inner, near]
                st[v, inner, ghost] = value
                st[v, inner, ghost2] = value
            for c in range(3):
                xs[c, inner, ghost] = 2.0 * xs[c, inner, near] - xs[c, inner, far]
                vs[c, inner, ghost] = vs[c, inner, near]
            sc[inner, ghost] = sc[inner, near]

        @pl.when(jnp.logical_not(at_end))
        def _():
            rad_states[side].wait_recv()
            rad_geometry[side].wait_recv()
            for i in range(tc):
                geometry(i + 2, ghost)

        primitives(inner, ghost)

    def rad_outer(step, carry):
        rad_face(step + (rc - 3) * (step // 2))
        return carry

    lax.fori_loop(0, 4, rad_outer, 0)

    for side in range(2):
        theta_geometry[side].wait_recv()
        theta_copies[side].wait_recv()

    def ghost_cells(step, carry):
        side, j = step // rc, step % rc
        for v in range(variables):
            for layer in range(2):
                start = ((side * variables + v) * instances * 2 + layer) * rc + j
                spread(halo_rows, start, v, side * (tc + 2) + layer, j + 2, 2 * rc)
        ghost = 1 + side * (tc + 1)
        geometry(ghost, j + 2)
        primitives(ghost, j + 2)
        return carry

    lax.fori_loop(0, 2 * rc, ghost_cells, 0)

    def theta_outer(step, carry):
        f = step // 2
        theta_face(f + (tc - 3) * (f // 2), step % 2)
        return carry

    lax.fori_loop(0, 8, theta_outer, 0)

    def finish(step, carry):
        v, i = step // tc, step % tc
        for j in range(rc):
            rows = pl.ds(v * plane + i * rc + j, instances, stride=lines)
            out_ref[rows, :] = out_ref[rows, :] + res[v, i + 2, j + 2, 0:instances]
        return carry

    lax.fori_loop(0, variables * tc, finish, 0)

    for copy in rad_copies + gather_copies + theta_copies + theta_geometry:
        copy.wait_send()

    @pl.when(rd < nr - 1)
    def _():
        rad_states[0].wait_send()
        rad_geometry[0].wait_send()

    @pl.when(rd > 0)
    def _():
        rad_states[1].wait_send()
        rad_geometry[1].wait_send()


def on_device(nt, nr, flow_state, face_scale, volume, surface, centre_index):
    variables, instances, tc, rc, na = flow_state.shape
    cen = centre_index.shape[0]
    sizes = (nt, nr, variables, instances, tc, rc, cen)
    table = jnp.asarray(constant_rows(instances, nt * tc))
    total = cen * nt * nr
    vmem = pl.BlockSpec(memory_space=pltpu.VMEM)
    f32 = jnp.float32
    cells = (tc + 4, rc + 4, 8, LANES)
    out = pl.pallas_call(
        functools.partial(kernel, sizes),
        out_shape=jax.ShapeDtypeStruct((variables * instances * tc * rc, na), f32),
        in_specs=[pl.BlockSpec(memory_space=pltpu.HBM)] * 6,
        out_specs=vmem,
        scratch_shapes=[
            pltpu.VMEM((variables * instances, tc * rc, na), f32),
            pltpu.VMEM((tc * rc, na), f32),
            pltpu.VMEM((tc * rc, na), f32),
            pltpu.VMEM(surface.shape, f32),
            pltpu.VMEM((1, cen), jnp.int32),
            pltpu.VMEM(table.shape, f32),
            pltpu.VMEM((nr, 16, LANES), f32),
            pltpu.VMEM((nt, 16, LANES), f32),
            pltpu.VMEM((16, total), jnp.bfloat16),
            pltpu.VMEM((tc * rc, total), f32),
            pltpu.VMEM((LANES, total), f32),
            pltpu.VMEM(cells, f32),
            pltpu.VMEM((5,) + cells, f32),
            pltpu.VMEM((4,) + cells, f32),
            pltpu.VMEM((3,) + cells, f32),
            pltpu.VMEM((3,) + cells, f32),
            pltpu.VMEM(cells, f32),
            pltpu.VMEM((5,) + cells, f32),
            pltpu.VMEM((2, variables * instances, 2 * rc, LANES), f32),
            pltpu.SemaphoreType.DMA((nr,)),
            pltpu.SemaphoreType.DMA((nr,)),
            pltpu.SemaphoreType.DMA((nt,)),
            pltpu.SemaphoreType.DMA((nt,)),
        ]
        + [pltpu.SemaphoreType.DMA((2,))] * 8
        + [pltpu.SemaphoreType.DMA((6,))],
        compiler_params=pltpu.CompilerParams(
            collective_id=0, has_side_effects=True, vmem_limit_bytes=64 * 1024 * 1024
        ),
    )(
        flow_state.reshape(variables * instances, tc * rc, na),
        face_scale.reshape(tc * rc, na),
        volume.reshape(tc * rc, na),
        surface,
        centre_index.reshape(1, cen),
        table,
    )
    return out.reshape(flow_state.shape)


def solution(mesh):
    return jax.shard_map(
        functools.partial(on_device, mesh.shape["theta"], mesh.shape["rad"]),
        mesh=mesh,
        in_specs=(
            P(None, None, "theta", "rad", None),
            P("theta", "rad", None),
            P("theta", "rad", None),
            P(None, ("theta", "rad")),
            P(("theta", "rad")),
        ),
        out_specs=P(None, None, "theta", "rad", None),
        check_vma=False,
    )
```

```python
import functools
import math

import jax
import jax.numpy as jnp
import numpy as np
from jax import lax
from jax.experimental import pallas as pl
from jax.experimental.pallas import tpu as pltpu
from jax.sharding import PartitionSpec as P

heat_ratio = 1.4
frequency = 0.8
damping = 0.0625
support_radius = 4.0
LANES = 128
MESH = pl.DeviceIdType.MESH


def derivative_table(instances):
    values = np.zeros((instances, instances))
    for row in range(instances):
        for col in range(instances):
            if row != col:
                steps = row - col
                values[row, col] = (
                    0.5 * frequency * (-1.0) ** steps / math.sin(math.pi * steps / instances)
                )
    return values


def constant_rows(instances, theta_total):
    phases = 2.0 * math.pi * np.arange(instances) / instances
    derivative = derivative_table(instances)
    rows = []
    for values in (np.cos(phases), np.sin(phases)):
        rows.append(np.resize(values, 8))
    for values in (np.cos(phases), np.sin(phases)):
        rows.append(np.resize(derivative @ values, 8))
    angle = 2.0 * math.pi / theta_total * (np.arange(theta_total) + 0.5)
    rows.append(np.cos(angle))
    rows.append(np.sin(angle))
    column = np.concatenate(rows).astype(np.float32)
    return np.ascontiguousarray(np.broadcast_to(column[:, None], (column.size, LANES)))


def dot3(a, b):
    return a[0] * b[0] + a[1] * b[1] + a[2] * b[2]


def face_flux(left, right, prim_l, prim_r, third, spacing, speed_sum, scale_sum):
    area = 0.5 * scale_sum
    factor = (0.5 * area) * lax.rsqrt(dot3(spacing, spacing))
    half = [s * factor for s in spacing]
    grid = 0.5 * dot3(speed_sum, half)
    un_l = dot3(prim_l, half)
    un_r = dot3(prim_r, half)
    q_l, q_r = un_l - grid, un_r - grid
    pressure = prim_l[3] + prim_r[3]
    flux = [left[v] * q_l + right[v] * q_r for v in range(5)]
    for c in range(3):
        flux[1 + c] = flux[1 + c] + pressure * half[c]
    flux[4] = flux[4] + prim_l[3] * un_l + prim_r[3] * un_r
    total = [left[v] + right[v] for v in range(5)]
    inverse = 1.0 / total[0]
    mean = [total[1 + c] * inverse for c in range(3)]
    sound2 = (heat_ratio * (heat_ratio - 1.0)) * (
        (total[4] - 0.5 * dot3(total[1:4], mean)) * inverse
    )
    spectral = 2.0 * jnp.abs(dot3(mean, half) - grid) + jnp.sqrt(sound2) * area
    weight = damping * spectral
    return [flux[v] + weight * third[v] for v in range(5)]


def end_flux(state, prim, third, spacing, speed, area):
    factor = area * lax.rsqrt(dot3(spacing, spacing))
    normal = [s * factor for s in spacing]
    un = dot3(prim, normal)
    q = un - dot3(speed, normal)
    flux = [state[v] * q for v in range(5)]
    for c in range(3):
        flux[1 + c] = flux[1 + c] + prim[3] * normal[c]
    flux[4] = flux[4] + prim[3] * un
    sound = jnp.sqrt(heat_ratio * prim[3] / state[0])
    weight = damping * (jnp.abs(q) + sound * area)
    return [flux[v] + weight * third[v] for v in range(5)]


def kernel(
    sizes,
    flow_in,
    scale_in,
    volume_in,
    surface_in,
    index_in,
    table_in,
    out_ref,
    flow_ref,
    scale_ref,
    volume_ref,
    surface_ref,
    index_ref,
    table_ref,
    own_pay,
    cent,
    weights,
    amat,
    bmat,
    hm,
    st,
    pr,
    xs,
    vs,
    sc,
    res,
    halo,
    gr_send,
    gr_recv,
    gt_send,
    gt_recv,
    st_send,
    st_recv,
    sr_send,
    sr_recv,
    ht_send,
    ht_recv,
    hr_send,
    hr_recv,
    in_sem,
):
    nt, nr, variables, instances, tc, rc, cen = sizes
    th = lax.axis_index("theta")
    rd = lax.axis_index("rad")
    up, down = lax.rem(th + 1, nt), lax.rem(th + nt - 1, nt)
    lines = tc * rc
    plane = instances * lines
    flow_rows = flow_ref.reshape(variables * plane, LANES)
    halo_rows = halo.reshape(2 * variables * instances * 2 * rc, LANES)
    hub = nt * tc / (2.0 * math.pi)

    inputs = [
        pltpu.make_async_copy(src, dst, in_sem.at[k])
        for k, (src, dst) in enumerate(
            (
                (surface_in, surface_ref),
                (index_in, index_ref),
                (flow_in, flow_ref),
                (volume_in, volume_ref),
                (table_in, table_ref),
                (scale_in, scale_ref),
            )
        )
    ]
    for copy in inputs:
        copy.start()
    barrier = pltpu.get_barrier_semaphore()
    for d in range(1, nr):
        pl.semaphore_signal(
            barrier, inc=1, device_id={"rad": lax.rem(rd + d, nr)}, device_id_type=MESH
        )
    for d in range(1, nt):
        pl.semaphore_signal(
            barrier, inc=1, device_id={"theta": lax.rem(th + d, nt)}, device_id_type=MESH
        )

    for copy in inputs[:2]:
        copy.wait()

    per = LANES // (cen * nr)
    offset = (lax.rem(th, per) * nr + rd) * cen
    nodes = surface_ref.shape[1]
    ids = index_ref[...] - (th * nr + rd) * nodes
    chosen = (lax.broadcasted_iota(jnp.int32, (nodes, cen), 0) == ids).astype(jnp.float32)
    placed = (
        lax.broadcasted_iota(jnp.int32, (cen, LANES), 1)
        == lax.broadcasted_iota(jnp.int32, (cen, LANES), 0) + offset
    ).astype(jnp.float32)
    pay = jnp.dot(
        surface_ref[...], chosen, precision=lax.Precision.HIGHEST, preferred_element_type=jnp.float32
    )
    pay = jnp.dot(
        pay, placed, precision=lax.Precision.HIGHEST, preferred_element_type=jnp.float32
    )
    own_pay[rd] = jnp.zeros((16, LANES), jnp.float32)
    own_pay[rd, 0:6] = pay[3:9]
    own_pay[rd, 8:11] = pay[0:3]

    pl.semaphore_wait(barrier, nr - 1 + nt - 1)

    def rad_gather(d):
        peer = lax.rem(rd + d, nr)
        return pltpu.make_async_remote_copy(
            src_ref=own_pay.at[rd],
            dst_ref=own_pay.at[rd],
            send_sem=gr_send.at[d],
            recv_sem=gr_recv.at[d],
            device_id={"rad": peer},
            device_id_type=MESH,
        )

    rad_copies = [rad_gather(d) for d in range(1, nr)]
    for copy in rad_copies:
        copy.start()

    def state_theta(side):
        src = flow_ref.at[:, pl.ds((tc - 2) * rc if side == 0 else 0, 2 * rc), :]
        return pltpu.make_async_remote_copy(
            src_ref=src,
            dst_ref=halo.at[side],
            send_sem=st_send.at[side],
            recv_sem=st_recv.at[side],
            device_id={"theta": up if side == 0 else down},
            device_id_type=MESH,
        )

    theta_copies = [state_theta(0), state_theta(1)]

    def spread(source, base, v, i, j, stride):
        st[v, i, j, 0:instances] = source[pl.ds(base, instances, stride=stride), :]
        st[v, i, j, instances : instances + 1] = source[pl.ds(base, 1), :]

    def own_rows(step, carry):
        v, i = step // tc, step % tc
        for j in range(rc):
            spread(flow_rows, v * plane + i * rc + j, v, i + 2, j + 2, lines)
        return carry

    for copy in inputs[2:]:
        copy.wait()
    for copy in rad_copies:
        copy.wait_recv()
    block = own_pay[0]
    for r in range(1, nr):
        block = block + own_pay[r]
    cent[th] = block

    def theta_gather(d):
        peer = lax.rem(th + d, nt)
        return pltpu.make_async_remote_copy(
            src_ref=cent.at[th],
            dst_ref=cent.at[th],
            send_sem=gt_send.at[d],
            recv_sem=gt_recv.at[d],
            device_id={"theta": peer},
            device_id_type=MESH,
        )

    gather_copies = [theta_gather(d) for d in range(1, nt)]
    for copy in gather_copies:
        copy.start()
    for copy in theta_copies:
        copy.start()

    lax.fori_loop(0, variables * tc, own_rows, 0)

    def state_rad(side):
        src = pl.ds(rc, 2) if side == 0 else pl.ds(2, 2)
        dst = pl.ds(0, 2) if side == 0 else pl.ds(rc + 2, 2)
        return pltpu.make_async_remote_copy(
            src_ref=st.at[:, pl.ds(2, tc), src],
            dst_ref=st.at[:, pl.ds(2, tc), dst],
            send_sem=sr_send.at[side],
            recv_sem=sr_recv.at[side],
            device_id={"rad": lax.rem(rd + 1, nr) if side == 0 else lax.rem(rd + nr - 1, nr)},
            device_id_type=MESH,
        )

    rad_states = [state_rad(0), state_rad(1)]

    @pl.when(rd < nr - 1)
    def _():
        rad_states[0].start()

    @pl.when(rd > 0)
    def _():
        rad_states[1].start()

    def primitives(i, j):
        u = [st[v, i, j] for v in range(5)]
        inverse = 1.0 / u[0]
        speed = [u[1 + c] * inverse for c in range(3)]
        for c in range(3):
            pr[c, i, j] = speed[c]
        pr[3, i, j] = (heat_ratio - 1.0) * (u[4] - 0.5 * dot3(u[1:4], speed))

    inner = pl.ds(2, tc)

    def own_prims(j, carry):
        primitives(inner, j + 2)
        for v in range(5):
            res[v, pl.ds(1, tc + 2), j + 2] = jnp.zeros((tc + 2, 8, LANES), jnp.float32)
        return carry

    lax.fori_loop(0, rc, own_prims, 0)
    for j in (1, rc + 2):
        for v in range(5):
            res[v, inner, j] = jnp.zeros((tc, 8, LANES), jnp.float32)

    derivative = derivative_table(instances)

    def temporal(step, carry):
        v, i = step // tc, step % tc
        vol = volume_ref[pl.ds(pl.multiple_of(i * rc, rc), rc), :]
        first = v * plane + i * rc
        parts = [
            vol * flow_rows[pl.ds(pl.multiple_of(first + n * lines, 8), rc), :]
            for n in range(instances)
        ]
        for n in range(instances):
            value = 0.0
            for s in range(1, (instances + 1) // 2):
                value = value + float(derivative[s, 0]) * (
                    parts[(n - s) % instances] - parts[(n + s) % instances]
                )
            out_ref[pl.ds(pl.multiple_of(first + n * lines, 8), rc), :] = value
        return carry

    lax.fori_loop(0, variables * tc, temporal, 0)

    for copy in gather_copies:
        copy.wait_recv()

    blocks = nt // per
    radius8 = (
        lax.broadcasted_iota(jnp.int32, (rc, LANES), 0) + rd * rc
    ).astype(jnp.float32) + (hub + 0.5)
    height = lax.broadcasted_iota(jnp.int32, (LANES, LANES), 0).astype(jnp.float32) + 0.5
    inv_h = 1.0 / support_radius
    for b in range(blocks):
        group = cent[b * per]
        for q in range(1, per):
            group = group + cent[b * per + q]
        cols = slice(b * LANES, (b + 1) * LANES)
        w = group[0:8]
        high = w.astype(jnp.bfloat16)
        low = (w - high.astype(jnp.float32)).astype(jnp.bfloat16)
        weights[:, cols] = jnp.concatenate([high, low], axis=0)
        cx, cy, cz = group[8:9], group[9:10], group[10:11]
        dz = (height - cz) * inv_h
        bmat[:, cols] = dz * dz
        for i in range(tc):
            row = 32 + th * tc + i
            cosine = table_ref[pl.ds(row, 1), :]
            sine = table_ref[pl.ds(row + nt * tc, 1), :]
            dx = (radius8 * cosine - cx) * inv_h
            dy = (radius8 * sine - cy) * inv_h
            amat[i * rc : (i + 1) * rc, cols] = 1.0 + (dx * dx + dy * dy)

    row8 = lax.broadcasted_iota(jnp.int32, (8, LANES), 0)
    width = 2 * LANES
    total = blocks * LANES

    def line_sum(i, j):
        line = i * rc + j
        acc = jnp.zeros((16, LANES), jnp.float32)
        for m in range(0, total, width):
            cols = slice(m, m + width)
            rbf = lax.rsqrt(amat[pl.ds(line, 1), cols] + bmat[:, cols])
            high = rbf.astype(jnp.bfloat16)
            low = (rbf - high.astype(jnp.float32)).astype(jnp.bfloat16)
            for part in (high, low):
                acc = acc + lax.dot_general(
                    weights[:, cols], part, (((1,), (1,)), ((), ())),
                    preferred_element_type=jnp.float32,
                )
        values = acc[0:8] + acc[8:16]
        hm[i + 2, j + 2] = jnp.where(row8 == 6, scale_ref[pl.ds(line, 1), :], values)

    def outer_lines(step, carry):
        line_sum((step // rc) * (tc - 1), step % rc)
        return carry

    lax.fori_loop(0, 2 * rc, outer_lines, 0)

    def geometry_theta(side):
        src = tc + 1 if side == 0 else 2
        dst = 1 if side == 0 else tc + 2
        return pltpu.make_async_remote_copy(
            src_ref=hm.at[src, pl.ds(2, rc)],
            dst_ref=hm.at[dst, pl.ds(2, rc)],
            send_sem=ht_send.at[side],
            recv_sem=ht_recv.at[side],
            device_id={"theta": up if side == 0 else down},
            device_id_type=MESH,
        )

    theta_geometry = [geometry_theta(0), geometry_theta(1)]
    for copy in theta_geometry:
        copy.start()

    def side_lines(step, carry):
        line_sum(1 + step // 2, (step % 2) * (rc - 1))
        return carry

    lax.fori_loop(0, 2 * (tc - 2), side_lines, 0)

    def geometry_rad(side):
        src = rc + 1 if side == 0 else 2
        dst = 1 if side == 0 else rc + 2
        return pltpu.make_async_remote_copy(
            src_ref=hm.at[pl.ds(2, tc), src],
            dst_ref=hm.at[pl.ds(2, tc), dst],
            send_sem=hr_send.at[side],
            recv_sem=hr_recv.at[side],
            device_id={"rad": lax.rem(rd + 1, nr) if side == 0 else lax.rem(rd + nr - 1, nr)},
            device_id_type=MESH,
        )

    rad_geometry = [geometry_rad(0), geometry_rad(1)]

    @pl.when(rd < nr - 1)
    def _():
        rad_geometry[0].start()

    @pl.when(rd > 0)
    def _():
        rad_geometry[1].start()

    def middle_lines(step, carry):
        line_sum(1 + step // (rc - 2), 1 + step % (rc - 2))
        return carry

    lax.fori_loop(0, (tc - 2) * (rc - 2), middle_lines, 0)

    axial = lax.broadcasted_iota(jnp.int32, (8, LANES), 1).astype(jnp.float32) + 0.5

    def geometry(i, j):
        wave = hm[i, j]
        rows = [jnp.broadcast_to(wave[c : c + 1], (8, LANES)) for c in range(7)]
        cell = lax.rem(th * tc + i - 2 + nt * tc, nt * tc)
        radius = (rd * rc + j - 2).astype(jnp.float32) + (hub + 0.5)
        base = (
            radius * table_ref[pl.ds(32 + cell, 1), :],
            radius * table_ref[pl.ds(32 + nt * tc + cell, 1), :],
            axial,
        )
        for c in range(3):
            xs[c, i, j] = base[c] + (rows[c] * table_ref[0:8] + rows[3 + c] * table_ref[8:16])
            vs[c, i, j] = rows[c] * table_ref[16:24] + rows[3 + c] * table_ref[24:32]
        sc[i, j] = rows[6]

    def own_geometry(j, carry):
        for i in range(tc):
            geometry(i + 2, j + 2)
        return carry

    lax.fori_loop(0, rc, own_geometry, 0)

    first = lax.broadcasted_iota(jnp.int32, (tc, 8, LANES), 2) == 0
    last = lax.broadcasted_iota(jnp.int32, (tc, 8, LANES), 2) == LANES - 1

    def before(x):
        return pltpu.roll(x, 1, axis=2)

    def after(x):
        return pltpu.roll(x, LANES - 1, axis=2)

    def axial_faces(step, carry):
        j = step + 2
        right = [st[v, inner, j] for v in range(5)]
        left = [jnp.where(first, x, before(x)) for x in right]
        change = [r - l for r, l in zip(right, left)]
        third = [after(d) - 2.0 * d + jnp.where(first, 0.0, before(d)) for d in change]
        prim_r = [pr[c, inner, j] for c in range(4)]
        prim_l = [jnp.where(first, x, before(x)) for x in prim_r]
        spacing = []
        for c in range(3):
            x = xs[c, inner, j]
            s = x - before(x)
            spacing.append(jnp.where(first, after(s), s))
        speed = [vs[c, inner, j] for c in range(3)]
        speed_sum = [x + jnp.where(first, x, before(x)) for x in speed]
        area = sc[inner, j]
        area_sum = area + jnp.where(first, area, before(area))
        lower = face_flux(left, right, prim_l, prim_r, third, spacing, speed_sum, area_sum)
        end = end_flux(right, prim_r, change, spacing, speed, area)
        for v in range(5):
            res[v, inner, j] += jnp.where(last, end[v], after(lower[v])) - lower[v]
        return carry

    lax.fori_loop(0, rc, axial_faces, 0)

    def faces(cells):
        ll, l, r, rr = cells
        left = [st[(v, *l)] for v in range(5)]
        right = [st[(v, *r)] for v in range(5)]
        third = [
            (st[(v, *rr)] - st[(v, *ll)]) - 3.0 * (right[v] - left[v]) for v in range(5)
        ]
        flux = face_flux(
            left,
            right,
            [pr[(c, *l)] for c in range(4)],
            [pr[(c, *r)] for c in range(4)],
            third,
            [xs[(c, *r)] - xs[(c, *l)] for c in range(3)],
            [vs[(c, *r)] + vs[(c, *l)] for c in range(3)],
            sc[l] + sc[r],
        )
        for v in range(5):
            res[(v, *l)] += flux[v]
            res[(v, *r)] -= flux[v]

    half = rc // 2

    def theta_face(f, part):
        j = pl.ds(2 + part * half, half)
        faces([(f + k, j) for k in range(4)])

    def rad_face(f):
        faces([(inner, f + k) for k in range(4)])

    def theta_inner(step, carry):
        theta_face(2 + step // 2, step % 2)
        return carry

    def rad_inner(step, carry):
        rad_face(2 + step)
        return carry

    lax.fori_loop(0, 2 * (tc - 3), theta_inner, 0)
    lax.fori_loop(0, rc - 3, rad_inner, 0)

    for side in range(2):
        near, far, ghost = (2, 3, 1) if side == 0 else (rc + 1, rc, rc + 2)
        ghost2 = 0 if side == 0 else rc + 3
        at_end = (rd == 0) if side == 0 else (rd == nr - 1)

        @pl.when(at_end)
        def _():
            for v in range(5):
                value = st[v, inner, near]
                st[v, inner, ghost] = value
                st[v, inner, ghost2] = value
            for c in range(3):
                xs[c, inner, ghost] = 2.0 * xs[c, inner, near] - xs[c, inner, far]
                vs[c, inner, ghost] = vs[c, inner, near]
            sc[inner, ghost] = sc[inner, near]

        @pl.when(jnp.logical_not(at_end))
        def _():
            rad_states[side].wait_recv()
            rad_geometry[side].wait_recv()
            for i in range(tc):
                geometry(i + 2, ghost)

        primitives(inner, ghost)

    def rad_outer(step, carry):
        rad_face(step + (rc - 3) * (step // 2))
        return carry

    lax.fori_loop(0, 4, rad_outer, 0)

    for side in range(2):
        theta_geometry[side].wait_recv()

    def ghost_geometry(step, carry):
        geometry(1 + (step // rc) * (tc + 1), step % rc + 2)
        return carry

    lax.fori_loop(0, 2 * rc, ghost_geometry, 0)

    for side in range(2):
        theta_copies[side].wait_recv()
        ghost = 1 + side * (tc + 1)
        early = tc // 2

        def ghost_cells(j, carry):
            for v in range(variables):
                for layer in range(2):
                    start = ((side * variables + v) * instances * 2 + layer) * rc + j
                    spread(halo_rows, start, v, side * (tc + 2) + layer, j + 2, 2 * rc)
            return carry

        lax.fori_loop(0, rc, ghost_cells, 0)
        for part in range(2):
            primitives(ghost, pl.ds(2 + part * half, half))

        def theta_outer(step, carry):
            theta_face(side * (tc - 1) + step // 2, step % 2)
            return carry

        lax.fori_loop(0, 4, theta_outer, 0)

        def finish(step, carry):
            v, i = step // early, side * early + step % early
            for j in range(rc):
                rows = pl.ds(v * plane + i * rc + j, instances, stride=lines)
                out_ref[rows, :] = out_ref[rows, :] + res[v, i + 2, j + 2, 0:instances]
            return carry

        lax.fori_loop(0, variables * early, finish, 0)

    for copy in rad_copies + gather_copies + theta_copies + theta_geometry:
        copy.wait_send()

    @pl.when(rd < nr - 1)
    def _():
        rad_states[0].wait_send()
        rad_geometry[0].wait_send()

    @pl.when(rd > 0)
    def _():
        rad_states[1].wait_send()
        rad_geometry[1].wait_send()


def on_device(nt, nr, flow_state, face_scale, volume, surface, centre_index):
    variables, instances, tc, rc, na = flow_state.shape
    cen = centre_index.shape[0]
    sizes = (nt, nr, variables, instances, tc, rc, cen)
    table = jnp.asarray(constant_rows(instances, nt * tc))
    total = cen * nt * nr
    vmem = pl.BlockSpec(memory_space=pltpu.VMEM)
    f32 = jnp.float32
    cells = (tc + 4, rc + 4, 8, LANES)
    out = pl.pallas_call(
        functools.partial(kernel, sizes),
        out_shape=jax.ShapeDtypeStruct((variables * instances * tc * rc, na), f32),
        in_specs=[pl.BlockSpec(memory_space=pltpu.HBM)] * 6,
        out_specs=vmem,
        scratch_shapes=[
            pltpu.VMEM((variables * instances, tc * rc, na), f32),
            pltpu.VMEM((tc * rc, na), f32),
            pltpu.VMEM((tc * rc, na), f32),
            pltpu.VMEM(surface.shape, f32),
            pltpu.VMEM((1, cen), jnp.int32),
            pltpu.VMEM(table.shape, f32),
            pltpu.VMEM((nr, 16, LANES), f32),
            pltpu.VMEM((nt, 16, LANES), f32),
            pltpu.VMEM((16, total), jnp.bfloat16),
            pltpu.VMEM((tc * rc, total), f32),
            pltpu.VMEM((LANES, total), f32),
            pltpu.VMEM(cells, f32),
            pltpu.VMEM((5,) + cells, f32),
            pltpu.VMEM((4,) + cells, f32),
            pltpu.VMEM((3,) + cells, f32),
            pltpu.VMEM((3,) + cells, f32),
            pltpu.VMEM(cells, f32),
            pltpu.VMEM((5,) + cells, f32),
            pltpu.VMEM((2, variables * instances, 2 * rc, LANES), f32),
            pltpu.SemaphoreType.DMA((nr,)),
            pltpu.SemaphoreType.DMA((nr,)),
            pltpu.SemaphoreType.DMA((nt,)),
            pltpu.SemaphoreType.DMA((nt,)),
        ]
        + [pltpu.SemaphoreType.DMA((2,))] * 8
        + [pltpu.SemaphoreType.DMA((6,))],
        compiler_params=pltpu.CompilerParams(
            collective_id=0, has_side_effects=True, vmem_limit_bytes=64 * 1024 * 1024
        ),
    )(
        flow_state.reshape(variables * instances, tc * rc, na),
        face_scale.reshape(tc * rc, na),
        volume.reshape(tc * rc, na),
        surface,
        centre_index.reshape(1, cen),
        table,
    )
    return out.reshape(flow_state.shape)


def solution(mesh):
    return jax.shard_map(
        functools.partial(on_device, mesh.shape["theta"], mesh.shape["rad"]),
        mesh=mesh,
        in_specs=(
            P(None, None, "theta", "rad", None),
            P("theta", "rad", None),
            P("theta", "rad", None),
            P(None, ("theta", "rad")),
            P(("theta", "rad")),
        ),
        out_specs=P(None, None, "theta", "rad", None),
        check_vma=False,
    )
```
